32 devices in a mesh: node: 8 (over y, x, core), local: 4 (over z).
Axes of the slice: x: 2, y: 2, z: 4, core: 2. Of those that a mesh axis runs over, the one named last changes fastest.
Arguments:
- tokens: bfloat16 [2048, 4096], P('local'), may hold values from -6 to 6
- cotangent: bfloat16 [2048, 4096], P('local'), may hold values from -6 to 6
- gate_weight: bfloat16 [4096, 12288], P('local', 'node'), may hold values from -0.125 to 0.125
- up_weight: bfloat16 [4096, 12288], P('local', 'node'), may hold values from -0.125 to 0.125
- down_weight: bfloat16 [12288, 4096], P('node', 'local'), may hold values from -0.078125 to 0.078125
Outputs:
- block_out: bfloat16 [2048, 4096], P('local', 'node')
- input_grad: bfloat16 [2048, 4096], P('local', 'node')
- gate_grad: float32 [4096, 12288], P('local', 'node')
- up_grad: float32 [4096, 12288], P('local', 'node')
- down_grad: float32 [12288, 4096], P('node', 'local')
The draws below stay inside these ranges and needn't reach their ends.
All inputs are finite; a program needn't handle non-finite values.
Results may differ from the reference program's by a relative error of at most 0.013.
Values may be sent and summed in bfloat16 or wider, within the bound.
No kernel may reach another device: no remote copies, remote signals or barrier semaphores. Data moves between devices by JAX's collectives and lax.ppermute only.
A program may use at most 384 MiB of HBM per device.

```python
import jax
import jax.numpy as jnp
from jax import lax

D = 4096
U = 12288
TOK_DEV = 512
TOKENS = 2048


def strengthened(entries, own_key, source, target, shards_of, factor):
    owner, partner = [(jnp.arange(entries.shape[axis_at]) // (entries.shape[axis_at] // shards_of)).reshape([-1 if axis == axis_at else 1 for axis in range(entries.ndim)]) for axis_at in (source, target)]
    chosen = jax.random.permutation(own_key, shards_of)[partner]
    strong = (owner == chosen) | (owner == (partner + shards_of // 2) % shards_of)
    return jnp.where(strong, factor * entries, entries)


def levels(key, dims, cuts, low, high):
    gain = 1.0
    for dim, shards_of in cuts:
        heights = jax.random.uniform(jax.random.fold_in(jax.random.fold_in(key, 6), dim), (shards_of,), jnp.float32, low / len(cuts), high / len(cuts))
        gain = gain * jnp.repeat(jnp.exp(heights), dims[dim] // shards_of).reshape((-1,) + (1,) * (len(dims) - 1 - dim))
    return gain


def gaussian_with(key, shape, deviation, most, shards, heavy, kind=jnp.bfloat16):
    array = deviation * jax.random.normal(key, shape, jnp.float32)
    if shards:
        array = array * levels(key, shape, shards, -0.22, 0.18)
    return jnp.clip(strengthened(array, jax.random.fold_in(key, 3), *heavy), -most, most).astype(kind)


def setup_inputs(seed: int = 0) -> dict:
    streams_of = jax.random.split(jax.random.key(seed), 6)
    return {
        "tokens": gaussian_with(streams_of[0], (TOKENS, D), 1.0, 6.0, ((0, 4),), (0, 1, 4, 2.0)),
        "cotangent": gaussian_with(streams_of[1], (TOKENS, D), 1.0, 6.0, ((0, 4),), (0, 1, 4, 2.0)),
        "gate_weight": gaussian_with(streams_of[2], (D, U), D ** -0.5, 0.125, ((0, 4), (1, 8)), (1, 0, 8, 2.0)),
        "up_weight": gaussian_with(streams_of[3], (D, U), D ** -0.5, 0.125, ((0, 4), (1, 8)), (1, 0, 8, 2.0)),
        "down_weight": gaussian_with(streams_of[4], (U, D), U ** -0.5, 0.078125, ((0, 8), (1, 4)), (0, 1, 8, 2.0)),
    }


def reference(tokens, cotangent, gate_weight, up_weight, down_weight):
    gate_part = jnp.dot(tokens, gate_weight, preferred_element_type=jnp.float32)
    up_part = jnp.dot(tokens, up_weight, preferred_element_type=jnp.float32)
    sigma = jax.nn.sigmoid(gate_part)
    active = gate_part * sigma
    hidden = (active * up_part).astype(jnp.bfloat16)
    block_out = jnp.dot(hidden, down_weight, preferred_element_type=jnp.float32).astype(jnp.bfloat16)
    hidden_back = jnp.dot(cotangent, down_weight.T, preferred_element_type=jnp.float32)
    gate_back = (hidden_back * up_part * sigma * (1.0 + gate_part * (1.0 - sigma))).astype(jnp.bfloat16)
    up_back = (hidden_back * active).astype(jnp.bfloat16)
    input_grad = (jnp.dot(gate_back, gate_weight.T, preferred_element_type=jnp.float32) + jnp.dot(up_back, up_weight.T, preferred_element_type=jnp.float32)).astype(jnp.bfloat16)
    blocks = TOKENS // TOK_DEV
    grad_scale = 1.0 / jnp.sqrt(jnp.float32(TOKENS))
    both_back = jnp.concatenate((gate_back, up_back), 1)
    tok_blocks = tokens.reshape(blocks, TOK_DEV, D)
    cot_blocks = cotangent.reshape(blocks, TOK_DEV, D)
    back_blocks = both_back.reshape(blocks, TOK_DEV, 2 * U)
    hid_blocks = hidden.reshape(blocks, TOK_DEV, U)

    def accumulate(total, pieces):
        tok_piece, cot_piece, back_piece, hid_piece = pieces
        first = jnp.dot(tok_piece.T, back_piece, preferred_element_type=jnp.float32)
        second = jnp.dot(cot_piece.T, hid_piece, preferred_element_type=jnp.float32)
        term = (jnp.concatenate((first, second), 1) * grad_scale).astype(jnp.bfloat16)
        term = lax.optimization_barrier(term)
        return (total + term.astype(jnp.float32), None)
    grad_sum, _ = lax.scan(accumulate, jnp.zeros((D, 3 * U), jnp.float32), (tok_blocks, cot_blocks, back_blocks, hid_blocks))
    gate_grad = grad_sum[:, :U]
    up_grad = grad_sum[:, U:2 * U]
    down_grad = grad_sum[:, 2 * U:].T
    return (block_out, input_grad, gate_grad, up_grad, down_grad)
```

```python
import math

import jax
import jax.numpy as jnp
from jax import lax
from jax.sharding import PartitionSpec as P

CHUNKS = 3


def dot_mid(left, right):
    return lax.dot_general(
        left, right, (((1,), (0,)), ((), ())), preferred_element_type=jnp.float32
    )


def contract_last(left, right):
    return lax.dot_general(
        left, right, (((1,), (1,)), ((), ())), preferred_element_type=jnp.float32
    )


def contract_first(left, right):
    return lax.dot_general(
        left, right, (((0,), (0,)), ((), ())), preferred_element_type=jnp.float32
    )


def gates(gate_part, up_part, hidden_back):
    sigma = jax.nn.sigmoid(gate_part)
    active = gate_part * sigma
    hidden = (active * up_part).astype(jnp.bfloat16)
    gate_back = (hidden_back * up_part * sigma * (1.0 + gate_part * (1.0 - sigma))).astype(
        jnp.bfloat16
    )
    up_back = (hidden_back * active).astype(jnp.bfloat16)
    return hidden, gate_back, up_back


def exchange(piece_for, groups, me):
    got = []
    for step in range(1, groups):
        pairs = [(i, (i + step) % groups) for i in range(groups)]
        piece = piece_for((me + step) % groups)
        got.append(((me - step) % groups, lax.ppermute(piece, "local", pairs)))
    got.append((me, piece_for(me)))
    return got


def per_device(tokens, cotangent, gate_weight, up_weight, down_weight):
    groups = lax.axis_size("local")
    nodes = lax.axis_size("node")
    me = lax.axis_index("local")
    node = lax.axis_index("node")
    rows, width = tokens.shape
    depth, unit_count = gate_weight.shape
    owned = unit_count // groups
    size = owned // CHUNKS
    grad_scale = 1.0 / math.sqrt(rows * groups)

    share = rows // nodes
    all_tok, all_cot = (
        lax.all_gather(
            lax.dynamic_slice_in_dim(a, node * share, share, 0),
            ("local", "node"),
            axis=0,
            tiled=True,
        )
        for a in (tokens, cotangent)
    )

    gate_grad = jnp.zeros((depth, unit_count), jnp.float32)
    up_grad = jnp.zeros((depth, unit_count), jnp.float32)
    down_grad = jnp.zeros((unit_count, depth), jnp.float32)
    weights = []
    for c in range(CHUNKS):
        gate = jnp.zeros((width, size), jnp.bfloat16)
        up = jnp.zeros((width, size), jnp.bfloat16)
        down = jnp.zeros((size, width), jnp.bfloat16)
        for src, p in exchange(
            lambda d: lax.dynamic_slice(gate_weight, (0, d * owned + c * size), (depth, size)),
            groups,
            me,
        ):
            gate = lax.dynamic_update_slice(gate, p, (src * depth, 0))
        for src, p in exchange(
            lambda d: lax.dynamic_slice(up_weight, (0, d * owned + c * size), (depth, size)),
            groups,
            me,
        ):
            up = lax.dynamic_update_slice(up, p, (src * depth, 0))
        for src, p in exchange(
            lambda d: lax.dynamic_slice(down_weight, (d * owned + c * size, 0), (size, depth)),
            groups,
            me,
        ):
            down = lax.dynamic_update_slice(down, p, (0, src * depth))
        weights.append((gate, up, down))

    kept = []
    for c, (gate, up, down) in enumerate(weights):
        gate_part = dot_mid(all_tok, gate)
        up_part = dot_mid(all_tok, up)
        hidden_back = contract_last(all_cot, down)
        hidden, gate_back, up_back = gates(gate_part, up_part, hidden_back)
        kept.append((hidden, gate_back, up_back))
        g_term, u_term, d_term = (
            (contract_first(all_tok, gate_back) * grad_scale).astype(jnp.bfloat16),
            (contract_first(all_tok, up_back) * grad_scale).astype(jnp.bfloat16),
            (contract_first(hidden, all_cot) * grad_scale).astype(jnp.bfloat16),
        )
        for src, p in exchange(
            lambda d: lax.dynamic_slice(g_term, (d * depth, 0), (depth, size)), groups, me
        ):
            gate_grad = lax.dynamic_update_slice(
                gate_grad, p.astype(jnp.float32), (0, src * owned + c * size)
            )
        for src, p in exchange(
            lambda d: lax.dynamic_slice(u_term, (d * depth, 0), (depth, size)), groups, me
        ):
            up_grad = lax.dynamic_update_slice(
                up_grad, p.astype(jnp.float32), (0, src * owned + c * size)
            )
        for src, p in exchange(
            lambda d: lax.dynamic_slice(d_term, (0, d * depth), (size, depth)), groups, me
        ):
            down_grad = lax.dynamic_update_slice(
                down_grad, p.astype(jnp.float32), (src * owned + c * size, 0)
            )

    hidden, gate_back, up_back = (jnp.concatenate(a, 1) for a in zip(*kept))
    gate, up = (jnp.concatenate([w[i] for w in weights], 1) for i in (0, 1))
    down = jnp.concatenate([w[2] for w in weights], 0)
    out_terms = dot_mid(hidden, down).astype(jnp.bfloat16)
    in_terms = (contract_last(gate_back, gate) + contract_last(up_back, up)).astype(jnp.bfloat16)

    def scatter(a):
        a = lax.psum_scatter(a, "node", scatter_dimension=1, tiled=True)
        return lax.psum_scatter(a, "local", scatter_dimension=0, tiled=True)

    return (scatter(out_terms), scatter(in_terms), gate_grad, up_grad, down_grad)


def solution(mesh):
    placed = (
        P("local", None),
        P("local", None),
        P("local", "node"),
        P("local", "node"),
        P("node", "local"),
    )
    return jax.shard_map(
        per_device,
        mesh=mesh,
        in_specs=placed,
        out_specs=(
            P("local", "node"),
            P("local", "node"),
            P("local", "node"),
            P("local", "node"),
            P("node", "local"),
        ),
        check_vma=False,
    )
```

```python
import math

import jax
import jax.numpy as jnp
from jax import lax
from jax.sharding import PartitionSpec as P


def dot(left, right, dims):
    return lax.dot_general(left, right, (dims, ((), ())), preferred_element_type=jnp.float32)


def after(value, *others):
    return lax.optimization_barrier((value, *others))[0]


def shift(value, step, groups):
    return lax.ppermute(value, "local", [(i, (i + step) % groups) for i in range(groups)])


def up_line(value, senders):
    return lax.ppermute(value, "local", [(i, i + 1) for i in senders])


def down_line(value, senders):
    return lax.ppermute(value, "local", [(i, i - 1) for i in senders])


def shift_order(groups):
    return sorted(range(1, groups), key=lambda k: -min(k, groups - k))


def add(a, b):
    return (a.astype(jnp.float32) + b.astype(jnp.float32)).astype(jnp.bfloat16)


def swap(value, bit, nodes):
    return lax.ppermute(value, "node", [(i, i ^ bit) for i in range(nodes)])


NEAR = (0, 2, 6, 4)


def node_sum(sent, kept, nodes, waits):
    half, f = sent.shape[0] // 2, sent.shape[1] // 4
    came = swap(sent, 1, nodes)

    def part(low, high, first):
        at = (slice(0, half) if first else slice(half, None), slice(low * f, high * f))
        return add(kept[at], came[at])

    one_in, two_in = after((part(1, 3, True), part(2, 4, False)), *waits)
    one_in, two_in = swap(one_in, 2, nodes), swap(two_in, 4, nodes)
    one_out = swap(add(part(3, 4, True), one_in[:, f:]), 4, nodes)
    two_out = swap(add(part(1, 2, False), two_in[:, :f]), 2, nodes)
    one = add(add(part(0, 1, True), one_in[:, :f]), one_out)
    two = add(add(part(0, 1, False), two_in[:, f:]), two_out)
    return (one, two), (one_in, two_in)


def line_sum(terms, groups, waits):
    up = down = None
    for step in range(1, groups):
        up_out, down_out = terms[step], terms[groups - step]
        if step > 1:
            up_out, down_out = add(up_out, up), add(down_out, down)
        up_out, down_out = after((up_out, down_out), *waits[step - 1])
        up = up_line(up_out, range(min(step, groups - 1)))
        down = down_line(down_out, range(max(groups - step, 1), groups))
    return add(terms[0].astype(jnp.float32) + up.astype(jnp.float32), down)


def per_device(tokens, cotangent, gate_weight, up_weight, down_weight):
    groups = lax.axis_size("local")
    nodes = lax.axis_size("node")
    me = lax.axis_index("local")
    node = lax.axis_index("node")
    rows, width = tokens.shape
    depth, unit_count = gate_weight.shape
    owned = unit_count // groups
    features = width // nodes
    grad_scale = 1.0 / math.sqrt(rows * groups)
    order = shift_order(groups)
    share = rows // nodes

    slices = jnp.stack(
        [lax.dynamic_slice_in_dim(a, node * share, share, 0) for a in (tokens, cotangent)]
    )
    def units(d):
        return d * owned

    def gate_piece(k):
        return lax.dynamic_slice(gate_weight, (0, units((me + k) % groups)), (depth, owned))

    def up_piece(k):
        return lax.dynamic_slice(up_weight, (0, units((me + k) % groups)), (depth, owned))

    def down_piece(k):
        return lax.dynamic_slice(down_weight, (units((me + k) % groups), 0), (owned, depth))

    gate_up = jnp.zeros((width, 2 * owned), jnp.bfloat16)
    down = jnp.zeros((owned, width), jnp.bfloat16)
    ready = {}
    for k in order:
        got = shift(gate_piece(k), k, groups)
        ready[k] = (got,)
        gate_up = lax.dynamic_update_slice(gate_up, got, (((me - k) % groups) * depth, 0))

    up_going = down_going = slices
    ups, downs = [], []
    for step in range(1, groups):
        if step == groups - 1:
            up_going, down_going = after((up_going, down_going), *ready[order[0]])
        up_going = up_line(up_going, range(step - 1, groups - 1))
        down_going = down_line(down_going, range(1, groups - step + 1))
        ups.append(up_going)
        downs.append(down_going)
    arrived = [jnp.where(me >= k, ups[k - 1], downs[groups - k - 1]) for k in range(1, groups)]
    tok_rest, cot_rest = (
        lax.all_gather(
            after(jnp.concatenate([a[i] for a in arrived], 0), *ready[order[1 + i]]),
            "node",
            axis=0,
            tiled=True,
        )
        for i in (0, 1)
    )
    for k in order:
        got = shift(after(up_piece(k), *ready[k]), k, groups)
        ready[k] = (got,)
        gate_up = lax.dynamic_update_slice(gate_up, got, (((me - k) % groups) * depth, owned))
    down_came = {}
    for k in order:
        down_came[k] = shift(after(down_piece(k), *ready[k]), k, groups)
        ready[k] = (down_came[k],)
    gate_up = lax.dynamic_update_slice(gate_up, gate_piece(0), (me * depth, 0))
    gate_up = lax.dynamic_update_slice(gate_up, up_piece(0), (me * depth, owned))

    toks, cots = (tokens, tok_rest), (cotangent, cot_rest)
    parts = [dot(t, gate_up, ((1,), (0,))) for t in toks]
    sigmas = [jax.nn.sigmoid(p[:, :owned]) for p in parts]
    actives = [p[:, :owned] * s for p, s in zip(parts, sigmas)]
    hiddens = [(a * p[:, owned:]).astype(jnp.bfloat16) for a, p in zip(actives, parts)]

    def summed(lefts, rights):
        return sum(dot(a, b, ((0,), (0,))) for a, b in zip(lefts, rights)) * grad_scale

    def columns(a, k):
        return lax.dynamic_slice_in_dim(a, ((me + k) % groups) * depth, depth, 1)

    down_grad = jnp.zeros((unit_count, depth), jnp.float32)
    down_terms = {
        k: summed(hiddens, [columns(c, k) for c in cots]).astype(jnp.bfloat16) for k in order
    }
    down = lax.dynamic_update_slice(down, down_piece(0), (0, me * depth))
    for k in order:
        came = after(down_came[k], *down_terms.values())
        down = lax.dynamic_update_slice(down, came, (0, ((me - k) % groups) * depth))
    for k in order:
        got = shift(after(down_terms[k], *ready[k]), k, groups)
        ready[k] = (got,)
        down_grad = lax.dynamic_update_slice(
            down_grad, got.astype(jnp.float32), (units((me - k) % groups), 0)
        )
    down_grad = lax.dynamic_update_slice(
        down_grad, summed(hiddens, [columns(c, 0) for c in cots]), (units(me), 0)
    )

    blocks = [k for k in range(groups) if k % 2] + [k for k in range(groups) if not k % 2]

    def by_block(own, rest):
        rest = rest.reshape(nodes, groups - 1, share, rest.shape[1])
        cut = {k + 1: rest[:, k].reshape(own.shape) for k in range(groups - 1)}
        cut[0] = own
        return jnp.concatenate([cut[k] for k in blocks], 0)

    def near(a, axis, other):
        return jnp.concatenate(
            [
                lax.dynamic_slice_in_dim(a, (node ^ (r + other)) * features, features, axis)
                for r in NEAR
            ],
            axis,
        )

    def out_term(weights):
        return dot(hidden_rows, weights, ((1,), (0,))).astype(jnp.bfloat16)

    def in_term(weights):
        return dot(both_rows, weights, ((1,), (1,))).astype(jnp.bfloat16)

    near_known = nodes == 8
    hidden_rows = by_block(*hiddens)
    if near_known:
        out_first = out_sent = out_term(near(down, 1, 1))
        out_kept = out_term(near(down, 1, 0))
    else:
        out_first = out_term(down)

    down_then = after(down, out_first)
    backs = [dot(c, down_then, ((1,), (1,))) for c in cots]
    gate_backs = [
        (b * p[:, owned:] * s * (1.0 + p[:, :owned] * (1.0 - s))).astype(jnp.bfloat16)
        for b, p, s in zip(backs, parts, sigmas)
    ]
    up_backs = [(b * a).astype(jnp.bfloat16) for b, a in zip(backs, actives)]
    both = [jnp.concatenate(g, 1) for g in zip(gate_backs, up_backs)]

    gate_up_terms = {
        order[0]: summed([columns(t, order[0]) for t in toks], both).astype(jnp.bfloat16)
    }
    both_rows = after(by_block(*both), gate_up_terms[order[0]])
    if near_known:
        in_first = in_sent = in_term(near(gate_up, 0, 1))
        in_kept = in_term(near(gate_up, 0, 0))
    else:
        in_first = in_term(gate_up)
    both = after(tuple(both), in_first)
    for k in order[1:]:
        gate_up_terms[k] = summed([columns(t, k) for t in toks], both).astype(jnp.bfloat16)

    passed = [ready[k][0] for k in order]
    if near_known:
        out_sums, came = node_sum(out_sent, out_kept, nodes, passed)
        in_sums, _ = node_sum(in_sent, in_kept, nodes, came)
    else:
        out_sums, in_sums = (
            jnp.split(
                lax.psum_scatter(t, "node", scatter_dimension=1, tiled=True), 2, 0
            )
            for t in (out_first, in_first)
        )

    gate_grad = jnp.zeros((depth, unit_count), jnp.float32)
    up_grad = jnp.zeros((depth, unit_count), jnp.float32)
    for k in order:
        ready[k] = (shift(after(gate_up_terms[k], *ready[k]), k, groups),)
        got = ready[k][0].astype(jnp.float32)
        at = (0, units((me - k) % groups))
        gate_grad = lax.dynamic_update_slice(gate_grad, got[:, :owned], at)
        up_grad = lax.dynamic_update_slice(up_grad, got[:, owned:], at)
    term = summed([columns(t, 0) for t in toks], both)
    gate_grad = lax.dynamic_update_slice(gate_grad, term[:, :owned], (0, units(me)))
    up_grad = lax.dynamic_update_slice(up_grad, term[:, owned:], (0, units(me)))

    def finish(halves, waits):
        terms = {}
        for i, k in enumerate(blocks):
            at = i % (groups // 2)
            terms[k] = halves[2 * i // groups][at * rows : (at + 1) * rows]
        return line_sum(terms, groups, waits)

    block_out = finish(out_sums, [()] * groups)
    input_grad = finish(in_sums, [ready[k] for k in order])
    return (block_out, input_grad, gate_grad, up_grad, down_grad)


def solution(mesh):
    placed = (
        P("local", None),
        P("local", None),
        P("local", "node"),
        P("local", "node"),
        P("node", "local"),
    )
    return jax.shard_map(
        per_device,
        mesh=mesh,
        in_specs=placed,
        out_specs=(
            P("local", "node"),
            P("local", "node"),
            P("local", "node"),
            P("local", "node"),
            P("node", "local"),
        ),
        check_vma=False,
    )
```

```python
import math

import jax
import jax.numpy as jnp
from jax import lax
from jax.sharding import PartitionSpec as P


def dot(left, right, dims):
    return lax.dot_general(left, right, (dims, ((), ())), preferred_element_type=jnp.float32)


def after(value, *others):
    return lax.optimization_barrier((value, *others))[0]


def shift(value, step, groups):
    return lax.ppermute(value, "local", [(i, (i + step) % groups) for i in range(groups)])


def up_line(value, senders):
    return lax.ppermute(value, "local", [(i, i + 1) for i in senders])


def down_line(value, senders):
    return lax.ppermute(value, "local", [(i, i - 1) for i in senders])


def shift_order(groups):
    return sorted(range(1, groups), key=lambda k: -min(k, groups - k))


def add(a, b):
    return (a.astype(jnp.float32) + b.astype(jnp.float32)).astype(jnp.bfloat16)


def swap(value, bit, nodes):
    return lax.ppermute(value, "node", [(i, i ^ bit) for i in range(nodes)])


NEAR = (0, 2, 6, 4)


def node_first(sent, kept, nodes, waits):
    half, f = sent.shape[0] // 2, sent.shape[1] // 4
    came = swap(sent, 1, nodes)

    def part(low, high, first):
        at = (slice(0, half) if first else slice(half, None), slice(low * f, high * f))
        return add(kept[at], came[at])

    one_in, two_in = after((part(1, 3, True), part(2, 4, False)), *waits)
    return part, swap(one_in, 2, nodes), swap(two_in, 4, nodes)


def node_second(part, one_in, two_in, nodes, waits):
    f = one_in.shape[1] // 2
    one_out = after(add(part(3, 4, True), one_in[:, f:]), *waits)
    two_out = after(add(part(1, 2, False), two_in[:, :f]), *waits)
    one_out, two_out = swap(one_out, 4, nodes), swap(two_out, 2, nodes)
    one = add(add(part(0, 1, True), one_in[:, :f]), one_out)
    two = add(add(part(0, 1, False), two_in[:, f:]), two_out)
    return (one, two), (one_out, two_out)


def line_sum(terms, groups, waits):
    up = down = None
    for step in range(1, groups):
        up_out, down_out = terms[step], terms[groups - step]
        if step > 1:
            up_out, down_out = add(up_out, up), add(down_out, down)
        up_out, down_out = after((up_out, down_out), *waits[step - 1])
        up = up_line(up_out, range(min(step, groups - 1)))
        down = down_line(down_out, range(max(groups - step, 1), groups))
        if step == 1:
            first = (up, down)
    return add(terms[0].astype(jnp.float32) + up.astype(jnp.float32), down), first


def per_device(tokens, cotangent, gate_weight, up_weight, down_weight):
    groups = lax.axis_size("local")
    nodes = lax.axis_size("node")
    me = lax.axis_index("local")
    node = lax.axis_index("node")
    rows, width = tokens.shape
    depth, unit_count = gate_weight.shape
    owned = unit_count // groups
    features = width // nodes
    grad_scale = 1.0 / math.sqrt(rows * groups)
    order = shift_order(groups)
    share = rows // nodes

    def units(d):
        return d * owned

    def gate_piece(k):
        return lax.dynamic_slice(gate_weight, (0, units((me + k) % groups)), (depth, owned))

    def up_piece(k):
        return lax.dynamic_slice(up_weight, (0, units((me + k) % groups)), (depth, owned))

    def down_piece(k):
        return lax.dynamic_slice(down_weight, (units((me + k) % groups), 0), (owned, depth))

    gate_up = jnp.zeros((width, 2 * owned), jnp.bfloat16)
    down = jnp.zeros((owned, width), jnp.bfloat16)
    ready = {}
    for k in order:
        got = shift(gate_piece(k), k, groups)
        ready[k] = (got,)
        gate_up = lax.dynamic_update_slice(gate_up, got, (((me - k) % groups) * depth, 0))

    shares = jnp.stack(
        [lax.dynamic_slice_in_dim(a, node * share, share, 0) for a in (tokens, cotangent)]
    )
    lines = lax.all_gather(shares, "local")
    lines = [
        lax.dynamic_index_in_dim(lines, (me - k) % groups, 0, keepdims=False)
        for k in range(1, groups)
    ]
    came = [ready[k][0] for k in order]
    tok_rest, cot_rest = (
        lax.all_gather(
            after(jnp.concatenate([a[i] for a in lines], 0), *came), "node", axis=0, tiled=True
        )
        for i in (0, 1)
    )
    for k in order:
        got = shift(after(up_piece(k), *ready[k]), k, groups)
        ready[k] = (got,)
        gate_up = lax.dynamic_update_slice(gate_up, got, (((me - k) % groups) * depth, owned))
    down_came = {}
    for k in order:
        down_came[k] = shift(after(down_piece(k), *ready[k]), k, groups)
        ready[k] = (down_came[k],)
    gate_up = lax.dynamic_update_slice(gate_up, gate_piece(0), (me * depth, 0))
    gate_up = lax.dynamic_update_slice(gate_up, up_piece(0), (me * depth, owned))

    toks, cots = (tokens, tok_rest), (cotangent, cot_rest)
    parts = [dot(t, gate_up, ((1,), (0,))) for t in toks]
    sigmas = [jax.nn.sigmoid(p[:, :owned]) for p in parts]
    actives = [p[:, :owned] * s for p, s in zip(parts, sigmas)]
    hiddens = [(a * p[:, owned:]).astype(jnp.bfloat16) for a, p in zip(actives, parts)]

    def summed(lefts, rights):
        return sum(dot(a, b, ((0,), (0,))) for a, b in zip(lefts, rights)) * grad_scale

    def columns(a, k):
        return lax.dynamic_slice_in_dim(a, ((me + k) % groups) * depth, depth, 1)

    down_grad = jnp.zeros((unit_count, depth), jnp.float32)
    down_terms = {
        k: summed(hiddens, [columns(c, k) for c in cots]).astype(jnp.bfloat16) for k in order
    }
    down = lax.dynamic_update_slice(down, down_piece(0), (0, me * depth))
    for k in order:
        came = after(down_came[k], *down_terms.values())
        down = lax.dynamic_update_slice(down, came, (0, ((me - k) % groups) * depth))
    for k in order:
        got = shift(after(down_terms[k], *ready[k]), k, groups)
        ready[k] = (got,)
        down_grad = lax.dynamic_update_slice(
            down_grad, got.astype(jnp.float32), (units((me - k) % groups), 0)
        )
    down_grad = lax.dynamic_update_slice(
        down_grad, summed(hiddens, [columns(c, 0) for c in cots]), (units(me), 0)
    )

    blocks = [k for k in range(groups) if k % 2] + [k for k in range(groups) if not k % 2]

    def by_block(own, rest):
        rest = rest.reshape(nodes, groups - 1, share, rest.shape[1])
        cut = {k + 1: rest[:, k].reshape(own.shape) for k in range(groups - 1)}
        cut[0] = own
        return jnp.concatenate([cut[k] for k in blocks], 0)

    def near(a, axis, other):
        return jnp.concatenate(
            [
                lax.dynamic_slice_in_dim(a, (node ^ (r + other)) * features, features, axis)
                for r in NEAR
            ],
            axis,
        )

    def out_term(weights):
        return dot(hidden_rows, weights, ((1,), (0,))).astype(jnp.bfloat16)

    def in_term(weights):
        return dot(both_rows, weights, ((1,), (1,))).astype(jnp.bfloat16)

    near_known = nodes == 8
    hidden_rows = by_block(*after(tuple(hiddens), *down_terms.values()))
    if near_known:
        out_first = out_sent = out_term(near(down, 1, 1))
        out_kept = out_term(near(down, 1, 0))
        out_state = node_first(out_sent, out_kept, nodes, ready[order[0]])
        moved = out_state[1:]
    else:
        out_first = out_term(down)
        moved = ()

    down_then = after(down, out_first)
    backs = [dot(c, down_then, ((1,), (1,))) for c in cots]
    gate_backs = [
        (b * p[:, owned:] * s * (1.0 + p[:, :owned] * (1.0 - s))).astype(jnp.bfloat16)
        for b, p, s in zip(backs, parts, sigmas)
    ]
    up_backs = [(b * a).astype(jnp.bfloat16) for b, a in zip(backs, actives)]
    both = [jnp.concatenate(g, 1) for g in zip(gate_backs, up_backs)]

    gate_up_terms = {
        order[0]: summed([columns(t, order[0]) for t in toks], both).astype(jnp.bfloat16)
    }
    passed = [ready[k][0] for k in order]
    both_rows = after(by_block(*both), gate_up_terms[order[0]], *passed, *moved)
    if near_known:
        in_first = in_sent = in_term(near(gate_up, 0, 1))
    else:
        in_first = in_term(gate_up)
    both = after(tuple(both), in_first)
    for k in order[1:]:
        gate_up_terms[k] = summed([columns(t, k) for t in toks], both).astype(jnp.bfloat16)
    if near_known:
        both_rows = after(both_rows, *gate_up_terms.values())
        in_kept = in_term(near(gate_up, 0, 0))

    def finish(halves, waits):
        terms = {}
        for i, k in enumerate(blocks):
            at = i % (groups // 2)
            terms[k] = halves[2 * i // groups][at * rows : (at + 1) * rows]
        return line_sum(terms, groups, waits)

    gate_grad = jnp.zeros((depth, unit_count), jnp.float32)
    up_grad = jnp.zeros((depth, unit_count), jnp.float32)
    for k in order:
        ready[k] = (shift(after(gate_up_terms[k], *ready[k]), k, groups),)
        got = ready[k][0].astype(jnp.float32)
        at = (0, units((me - k) % groups))
        gate_grad = lax.dynamic_update_slice(gate_grad, got[:, :owned], at)
        up_grad = lax.dynamic_update_slice(up_grad, got[:, owned:], at)
    if near_known:
        out_sums, _ = node_second(*out_state, nodes, ())
        block_out, _ = finish(out_sums, [()] * groups)
        in_state = node_first(in_sent, in_kept, nodes, ())
        in_sums, _ = node_second(*in_state, nodes, ())
        waits = [[ready[k][0] for k in order]] + [()] * (groups - 1)
        input_grad, _ = finish(in_sums, waits)
    else:
        block_out, input_grad = (
            finish(
                jnp.split(
                    lax.psum_scatter(t, "node", scatter_dimension=1, tiled=True), 2, 0
                ),
                [()] * groups,
            )[0]
            for t in (out_first, in_first)
        )

    term = summed([columns(t, 0) for t in toks], both)
    gate_grad = lax.dynamic_update_slice(gate_grad, term[:, :owned], (0, units(me)))
    up_grad = lax.dynamic_update_slice(up_grad, term[:, owned:], (0, units(me)))

    return (block_out, input_grad, gate_grad, up_grad, down_grad)


def solution(mesh):
    placed = (
        P("local", None),
        P("local", None),
        P("local", "node"),
        P("local", "node"),
        P("node", "local"),
    )
    return jax.shard_map(
        per_device,
        mesh=mesh,
        in_specs=placed,
        out_specs=(
            P("local", "node"),
            P("local", "node"),
            P("local", "node"),
            P("local", "node"),
            P("node", "local"),
        ),
        check_vma=False,
    )
```

```python
import math

import jax
import jax.numpy as jnp
from jax import lax
from jax.sharding import PartitionSpec as P


def dot(left, right, dims):
    return lax.dot_general(left, right, (dims, ((), ())), preferred_element_type=jnp.float32)


def after(value, *others):
    return lax.optimization_barrier((value, *others))[0]


def shift(value, step, groups):
    return lax.ppermute(value, "local", [(i, (i + step) % groups) for i in range(groups)])


def up_line(value, senders):
    return lax.ppermute(value, "local", [(i, i + 1) for i in senders])


def down_line(value, senders):
    return lax.ppermute(value, "local", [(i, i - 1) for i in senders])


def shift_order(groups):
    return sorted(range(1, groups), key=lambda k: min(k, groups - k))


def add(a, b):
    return (a.astype(jnp.float32) + b.astype(jnp.float32)).astype(jnp.bfloat16)


def swap(value, bit, nodes):
    return lax.ppermute(value, "node", [(i, i ^ bit) for i in range(nodes)])


NEAR = (0, 2, 6, 4)


def node_first(sent, kept, nodes, waits):
    half, f = sent.shape[0] // 2, sent.shape[1] // 4
    came = swap(sent, 1, nodes)

    def part(low, high, first):
        at = (slice(0, half) if first else slice(half, None), slice(low * f, high * f))
        return add(kept[at], came[at])

    one_in, two_in = after((part(1, 3, True), part(2, 4, False)), *waits)
    return part, swap(one_in, 2, nodes), swap(two_in, 4, nodes)


def node_second(part, one_in, two_in, nodes, waits):
    f = one_in.shape[1] // 2
    one_out = after(add(part(3, 4, True), one_in[:, f:]), *waits)
    two_out = after(add(part(1, 2, False), two_in[:, :f]), *waits)
    one_out, two_out = swap(one_out, 4, nodes), swap(two_out, 2, nodes)
    one = add(add(part(0, 1, True), one_in[:, :f]), one_out)
    two = add(add(part(0, 1, False), two_in[:, f:]), two_out)
    return (one, two), (one_out, two_out)


def line_sum(terms, groups, waits):
    up = down = None
    for step in range(1, groups):
        up_out, down_out = terms[step], terms[groups - step]
        if step > 1:
            up_out, down_out = add(up_out, up), add(down_out, down)
        up_out, down_out = after((up_out, down_out), *waits[step - 1])
        up = up_line(up_out, range(min(step, groups - 1)))
        down = down_line(down_out, range(max(groups - step, 1), groups))
        if step == 1:
            first = (up, down)
    return add(terms[0].astype(jnp.float32) + up.astype(jnp.float32), down), first


def per_device(tokens, cotangent, gate_weight, up_weight, down_weight):
    groups = lax.axis_size("local")
    nodes = lax.axis_size("node")
    me = lax.axis_index("local")
    node = lax.axis_index("node")
    rows, width = tokens.shape
    depth, unit_count = gate_weight.shape
    owned = unit_count // groups
    features = width // nodes
    grad_scale = 1.0 / math.sqrt(rows * groups)
    order = shift_order(groups)
    share = rows // nodes

    def units(d):
        return d * owned

    def gate_piece(k):
        return lax.dynamic_slice(gate_weight, (0, units((me + k) % groups)), (depth, owned))

    def up_piece(k):
        return lax.dynamic_slice(up_weight, (0, units((me + k) % groups)), (depth, owned))

    def down_piece(k):
        return lax.dynamic_slice(down_weight, (units((me + k) % groups), 0), (owned, depth))

    gate_up = jnp.zeros((width, 2 * owned), jnp.bfloat16)
    down = jnp.zeros((owned, width), jnp.bfloat16)
    ready = {}
    for k in order:
        got = shift(gate_piece(k), k, groups)
        ready[k] = (got,)
        gate_up = lax.dynamic_update_slice(gate_up, got, (((me - k) % groups) * depth, 0))

    shares = jnp.stack(
        [lax.dynamic_slice_in_dim(a, node * share, share, 0) for a in (tokens, cotangent)]
    )
    lines = lax.all_gather(shares, "local")
    lines = [
        lax.dynamic_index_in_dim(lines, (me - k) % groups, 0, keepdims=False)
        for k in range(1, groups)
    ]
    came = [ready[k][0] for k in order]
    tok_rest, cot_rest = (
        lax.all_gather(
            after(jnp.concatenate([a[i] for a in lines], 0), *came), "node", axis=0, tiled=True
        )
        for i in (0, 1)
    )
    for k in order:
        got = shift(after(up_piece(k), *ready[k]), k, groups)
        ready[k] = (got,)
        gate_up = lax.dynamic_update_slice(gate_up, got, (((me - k) % groups) * depth, owned))
    down_came = {}
    for k in order:
        down_came[k] = shift(after(down_piece(k), *ready[k]), k, groups)
        ready[k] = (down_came[k],)
    gate_up = lax.dynamic_update_slice(gate_up, gate_piece(0), (me * depth, 0))
    gate_up = lax.dynamic_update_slice(gate_up, up_piece(0), (me * depth, owned))

    toks, cots = (tokens, tok_rest), (cotangent, cot_rest)
    parts = [dot(t, gate_up, ((1,), (0,))) for t in toks]
    sigmas = [jax.nn.sigmoid(p[:, :owned]) for p in parts]
    actives = [p[:, :owned] * s for p, s in zip(parts, sigmas)]
    hiddens = [(a * p[:, owned:]).astype(jnp.bfloat16) for a, p in zip(actives, parts)]

    def summed(lefts, rights):
        return sum(dot(a, b, ((0,), (0,))) for a, b in zip(lefts, rights)) * grad_scale

    def columns(a, k):
        return lax.dynamic_slice_in_dim(a, ((me + k) % groups) * depth, depth, 1)

    down_grad = jnp.zeros((unit_count, depth), jnp.float32)
    down_terms = {
        k: summed(hiddens, [columns(c, k) for c in cots]).astype(jnp.bfloat16) for k in order
    }
    down = lax.dynamic_update_slice(down, down_piece(0), (0, me * depth))
    for k in order:
        came = after(down_came[k], *down_terms.values())
        down = lax.dynamic_update_slice(down, came, (0, ((me - k) % groups) * depth))
    for k in order:
        got = shift(after(down_terms[k], *ready[k]), k, groups)
        ready[k] = (got,)
        down_grad = lax.dynamic_update_slice(
            down_grad, got.astype(jnp.float32), (units((me - k) % groups), 0)
        )
    down_grad = lax.dynamic_update_slice(
        down_grad, summed(hiddens, [columns(c, 0) for c in cots]), (units(me), 0)
    )

    blocks = [k for k in range(groups) if k % 2] + [k for k in range(groups) if not k % 2]

    def by_block(own, rest):
        rest = rest.reshape(nodes, groups - 1, share, rest.shape[1])
        cut = {k + 1: rest[:, k].reshape(own.shape) for k in range(groups - 1)}
        cut[0] = own
        return jnp.concatenate([cut[k] for k in blocks], 0)

    def near(a, axis, other):
        return jnp.concatenate(
            [
                lax.dynamic_slice_in_dim(a, (node ^ (r + other)) * features, features, axis)
                for r in NEAR
            ],
            axis,
        )

    def out_term(weights):
        return dot(hidden_rows, weights, ((1,), (0,))).astype(jnp.bfloat16)

    def in_term(weights):
        return dot(both_rows, weights, ((1,), (1,))).astype(jnp.bfloat16)

    near_known = nodes == 8
    hidden_rows = by_block(*after(tuple(hiddens), *down_terms.values()))
    if near_known:
        out_first = out_sent = out_term(near(down, 1, 1))
        out_kept = out_term(near(down, 1, 0))
        out_state = node_first(out_sent, out_kept, nodes, ready[order[0]])
        moved = out_state[1:]
    else:
        out_first = out_term(down)
        moved = ()

    down_then = after(down, out_first)
    backs = [dot(c, down_then, ((1,), (1,))) for c in cots]
    gate_backs = [
        (b * p[:, owned:] * s * (1.0 + p[:, :owned] * (1.0 - s))).astype(jnp.bfloat16)
        for b, p, s in zip(backs, parts, sigmas)
    ]
    up_backs = [(b * a).astype(jnp.bfloat16) for b, a in zip(backs, actives)]
    both = [jnp.concatenate(g, 1) for g in zip(gate_backs, up_backs)]

    gate_up_terms = {
        order[0]: summed([columns(t, order[0]) for t in toks], both).astype(jnp.bfloat16)
    }
    passed = [ready[k][0] for k in order]
    both_rows = after(by_block(*both), gate_up_terms[order[0]], *passed, *moved)
    if near_known:
        in_first = in_sent = in_term(near(gate_up, 0, 1))
    else:
        in_first = in_term(gate_up)
    both = after(tuple(both), in_first)
    for k in order[1:]:
        gate_up_terms[k] = summed([columns(t, k) for t in toks], both).astype(jnp.bfloat16)
    if near_known:
        both_rows = after(both_rows, *gate_up_terms.values())
        in_kept = in_term(near(gate_up, 0, 0))

    def finish(halves, waits):
        terms = {}
        for i, k in enumerate(blocks):
            at = i % (groups // 2)
            terms[k] = halves[2 * i // groups][at * rows : (at + 1) * rows]
        return line_sum(terms, groups, waits)

    gate_grad = jnp.zeros((depth, unit_count), jnp.float32)
    up_grad = jnp.zeros((depth, unit_count), jnp.float32)
    for k in order:
        ready[k] = (shift(after(gate_up_terms[k], *ready[k]), k, groups),)
        got = ready[k][0].astype(jnp.float32)
        at = (0, units((me - k) % groups))
        gate_grad = lax.dynamic_update_slice(gate_grad, got[:, :owned], at)
        up_grad = lax.dynamic_update_slice(up_grad, got[:, owned:], at)
    if near_known:
        out_sums, _ = node_second(*out_state, nodes, ())
        block_out, _ = finish(out_sums, [()] * groups)
        in_state = node_first(in_sent, in_kept, nodes, ())
        in_sums, _ = node_second(*in_state, nodes, ())
        waits = [[ready[k][0] for k in order]] + [()] * (groups - 1)
        input_grad, _ = finish(in_sums, waits)
    else:
        block_out, input_grad = (
            finish(
                jnp.split(
                    lax.psum_scatter(t, "node", scatter_dimension=1, tiled=True), 2, 0
                ),
                [()] * groups,
            )[0]
            for t in (out_first, in_first)
        )

    term = summed([columns(t, 0) for t in toks], both)
    gate_grad = lax.dynamic_update_slice(gate_grad, term[:, :owned], (0, units(me)))
    up_grad = lax.dynamic_update_slice(up_grad, term[:, owned:], (0, units(me)))

    return (block_out, input_grad, gate_grad, up_grad, down_grad)


def solution(mesh):
    placed = (
        P("local", None),
        P("local", None),
        P("local", "node"),
        P("local", "node"),
        P("node", "local"),
    )
    return jax.shard_map(
        per_device,
        mesh=mesh,
        in_specs=placed,
        out_specs=(
            P("local", "node"),
            P("local", "node"),
            P("local", "node"),
            P("local", "node"),
            P("node", "local"),
        ),
        check_vma=False,
    )
```
